768 devices in a mesh: aux: 64 (over y, x, core), occ: 12 (over z).
Axes of the slice: x: 4, y: 8, z: 12, core: 2. Of those that a mesh axis runs over, the one named last changes fastest.
Arguments:
- aux_tiles: bfloat16 [256, 64, 128, 128], P('aux'), may hold values from -0.5 to 0.5
- orbitals: bfloat16 [48, 5376], P('occ'), may hold values from -0.29882812 to 0.29882812
- tile_rows: int32 [64, 64], P('aux'), may hold values from 0 to 41, as said below
- tile_cols: int32 [64, 64], P('aux'), may hold values from 0 to 41
- tile_count: int32 [64], P('aux'), may hold values from 42 to 64, as said below
Outputs:
- exchange: float32 [5376, 5376], P('aux', 'occ')
The draws below stay inside these ranges and needn't reach their ends.
Inputs may be any that keep to these rules, and one draw needn't show every extreme that they name: `tile_rows`: in every slab the first 42 slots name each row block once. `tile_count`: some slab has all 64 slots live and some slab exactly 42.
All inputs are finite; a program needn't handle non-finite values.
Results may differ from the reference program's by a relative error of at most 0.0027.
Values may be sent and summed in bfloat16 or wider, within the bound.
A program may use at most 64 MiB of HBM per device.

```python
import jax
import jax.numpy as jnp
from jax import lax

TILE = 128
NB = 42
NT = 64
P_DEV = 4
NBF = 5376
NAUX = 256
OCC = 48
N_AUX = 64


def draw_tile_rows(key, part):
    key = jax.random.fold_in(key, 11)
    first_key, second_key = jax.random.split(key)
    slab_keys = jax.random.split(first_key, N_AUX)
    covered = jax.vmap(lambda k: jax.random.permutation(k, NB))(slab_keys).astype(jnp.int32)
    extra = jax.random.randint(second_key, (N_AUX, NT - NB), 0, NB, dtype=jnp.int32)
    return jnp.concatenate([covered, extra], axis=1)


def draw_tile_cols(key, part):
    key = jax.random.fold_in(key, 12)
    return jax.random.randint(key, (N_AUX, NT), 0, NB, dtype=jnp.int32)


def draw_tile_count(key, part):
    key = jax.random.fold_in(key, 13)
    base_key, first_key, second_key = jax.random.split(key, 3)
    counts = jax.random.randint(base_key, (N_AUX,), NB, NT + 1, dtype=jnp.int32)
    full_slab = jax.random.randint(first_key, (), 0, N_AUX, dtype=jnp.int32)
    least_slab = (full_slab + 1 + jax.random.randint(second_key, (), 0, N_AUX - 1, dtype=jnp.int32)) % N_AUX
    counts = counts.at[full_slab].set(NT)
    return counts.at[least_slab].set(NB)


def shard_levels(rng, dims, cuts, low, largest):
    level = 1.0
    for position, parts in cuts:
        heights = jax.random.uniform(jax.random.fold_in(jax.random.fold_in(rng, 6), position), (parts,), jnp.float32, low / len(cuts), largest / len(cuts))
        level = level * jnp.repeat(jnp.exp(heights), dims[position] // parts).reshape((-1,) + (1,) * (len(dims) - 1 - position))
    return level


def normal_values(rng, shape, deviation, limit, pieces=(), kind=jnp.bfloat16):
    loudness = shard_levels(rng, shape, pieces, -0.22, 0.18) if pieces else 1.0
    drawn = jax.random.normal(rng, shape, jnp.float32) * deviation * loudness
    return jnp.minimum(jnp.maximum(drawn, -limit), limit).astype(kind)


def setup_inputs(seed: int = 0) -> dict:
    streams_of = jax.random.split(jax.random.key(seed), 6)
    return {
        "aux_tiles": normal_values(streams_of[0], (NAUX, NT, TILE, TILE), TILE ** -0.5, 0.5, ((0, 64),)),
        "orbitals": normal_values(streams_of[1], (OCC, NBF), 0.05, 0.29882812, ((0, 12),)),
        "tile_rows": draw_tile_rows(jax.random.fold_in(streams_of[5], 71), 0),
        "tile_cols": draw_tile_cols(jax.random.fold_in(streams_of[5], 71), 0),
        "tile_count": draw_tile_count(jax.random.fold_in(streams_of[5], 71), 0),
    }


def slab_half(blocks, rows_list, cols_list, live_count, orbitals):
    orb_blocks = orbitals.reshape(OCC, NB, TILE)[:, cols_list, :]
    half_tile = jnp.einsum("ptmn,itn->itpm", blocks.astype(jnp.float32), orb_blocks.astype(jnp.float32))
    live_tiles = (jnp.arange(NT, dtype=jnp.int32) < live_count).astype(jnp.float32)
    onehot = (rows_list[:, None] == jnp.arange(NB, dtype=jnp.int32)[None, :]).astype(jnp.float32) * live_tiles[:, None]
    placed = jnp.einsum("tb,itpm->ipbm", onehot, half_tile, precision=lax.Precision.HIGHEST)
    return placed.reshape(OCC, P_DEV, NBF).astype(jnp.bfloat16)


def reference(aux_tiles, orbitals, tile_rows, tile_cols, tile_count):
    grouped = aux_tiles.reshape(N_AUX, P_DEV, NT, TILE, TILE)

    def one_slab(args):
        return slab_half(args[0], args[1], args[2], args[3], orbitals)

    halves = lax.map(one_slab, (grouped, tile_rows, tile_cols, tile_count))
    flat = jnp.transpose(halves, (1, 0, 2, 3)).reshape(OCC * NAUX, NBF)
    return jnp.dot(flat.T, flat, preferred_element_type=jnp.float32)
```

```python
import functools

import jax
import jax.numpy as jnp
from jax import lax
from jax.experimental import pallas as pl
from jax.experimental.pallas import tpu as pltpu
from jax.sharding import PartitionSpec as P

MESH = pl.DeviceIdType.MESH
TILE = 128
NB = 42
NT = 64
PD = 4
OL = 4
BASIS = NB * TILE
NX, NY, NC, NZ = 4, 8, 2, 12
ROWS = 84
COLS = 448
SEG = COLS // NX
GROUP = (64, 48)
LANES = (768, 640)
BASE = (0, 768)
XW = 1408
YH = 384
YW = 2 * YH
KP = PD * OL
SLOTS_STEP = 8


def half_kernel(rows_ref, cols_ref, count_ref, tiles_ref, orb_ref, hx_ref, hy_ref, acc, flat):
    step = pl.program_id(0)

    @pl.when(step == 0)
    def _():
        acc[...] = jnp.zeros_like(acc)

    for s in range(SLOTS_STEP):
        t = step * SLOTS_STEP + s
        row = rows_ref[0, t]
        col = cols_ref[0, t]
        block = orb_ref[:, pl.ds(pl.multiple_of(col * TILE, TILE), TILE)]
        tile = tiles_ref[:, s].reshape(PD * TILE, TILE)
        got = lax.dot_general(block, tile, (((1,), (1,)), ((), ())), preferred_element_type=jnp.float32)
        live = (t < count_ref[0]).astype(jnp.float32)
        acc[row] += got * live

    @pl.when(step == pl.num_programs(0) - 1)
    def _():
        for b in range(NB):
            for p in range(PD):
                flat[p * OL:(p + 1) * OL, b * TILE:(b + 1) * TILE] = acc[b, :, p * TILE:(p + 1) * TILE]
        for x in range(NX):
            parts = []
            for g, start in ((0, 0), (1, GROUP[0])):
                for o in range(NZ):
                    a = o * COLS + x * SEG + start
                    parts.append(flat[:, a:a + GROUP[g]])
            parts.append(jnp.zeros((KP, XW - NZ * SEG), jnp.float32))
            hx_ref[x] = jnp.concatenate(parts, axis=1).astype(jnp.bfloat16)
        for y in range(NY):
            parts = []
            for c in range(NC):
                for x in range(NX):
                    a = ((y * NX + x) * NC + c) * ROWS
                    parts.append(flat[:, a:a + ROWS])
                parts.append(jnp.zeros((KP, YH - NX * ROWS), jnp.float32))
            hy_ref[y] = jnp.concatenate(parts, axis=1).astype(jnp.bfloat16)


def half(aux_tiles, orbitals, tile_rows, tile_cols, tile_count):
    smem = pl.BlockSpec(memory_space=pltpu.SMEM)
    return pl.pallas_call(
        half_kernel,
        grid=(NT // SLOTS_STEP,),
        in_specs=[
            smem, smem, smem,
            pl.BlockSpec((PD, SLOTS_STEP, TILE, TILE), lambda i: (0, i, 0, 0)),
            pl.BlockSpec((OL, BASIS), lambda i: (0, 0)),
        ],
        out_specs=[
            pl.BlockSpec((NX, KP, XW), lambda i: (0, 0, 0)),
            pl.BlockSpec((NY, KP, YW), lambda i: (0, 0, 0)),
        ],
        out_shape=[
            jax.ShapeDtypeStruct((NX, KP, XW), jnp.bfloat16),
            jax.ShapeDtypeStruct((NY, KP, YW), jnp.bfloat16),
        ],
        scratch_shapes=[
            pltpu.VMEM((NB, OL, PD * TILE), jnp.float32),
            pltpu.VMEM((KP, BASIS), jnp.float32),
        ],
        compiler_params=pltpu.CompilerParams(vmem_limit_bytes=32 * 2**20),
    )(tile_rows, tile_cols, tile_count, aux_tiles, orbitals)


def exchange_kernel(
    hx_ref, hy_ref, out_ref,
    hx, hy, part, own, sib_out, sib_in, minus_out, minus_in, plus_out, plus_in, final_out, final_in,
    local_sem, x_send, x_recv, y_send, y_recv, ring_send, ring_recv, row_send, row_recv,
    sib_send, sib_recv, minus_send, minus_recv, plus_send, plus_recv, fin_send, fin_recv,
):
    aux = lax.axis_index("aux")
    z = lax.axis_index("occ")
    c = lax.rem(aux, NC)
    x = lax.rem(aux // NC, NX)
    y = aux // (NC * NX)

    def at(y_, x_, c_, z_):
        return ((y_ * NX + x_) * NC + c_, z_)

    def xp(d):
        return lax.rem(x + d, NX)

    def yp(d):
        return lax.rem(y + d, NY)

    def zp(d):
        return lax.rem(z + d, NZ)

    partners = [at(y, xp(d), c, z) for d in range(1, NX)]
    partners += [at(yp(d), x, c, z) for d in range(1, NY)]
    partners += [at(y, x, 1 - c, z), at(y, x, c, zp(1)), at(y, x, c, zp(NZ - 1))]
    barrier = pltpu.get_barrier_semaphore()
    for partner in partners:
        pl.semaphore_signal(barrier, inc=1, device_id=partner, device_id_type=MESH)
    pl.semaphore_wait(barrier, len(partners))

    waits = []

    def send(src, dst, s_sem, r_sem, device):
        copy = pltpu.make_async_remote_copy(
            src_ref=src, dst_ref=dst, send_sem=s_sem, recv_sem=r_sem, device_id=device, device_id_type=MESH)
        copy.start()
        waits.append(copy)
        return copy

    own_x = pltpu.make_async_copy(hx_ref.at[x], hx.at[y, x], local_sem.at[0])
    own_y = pltpu.make_async_copy(hy_ref.at[y], hy.at[y, x], local_sem.at[1])
    own_x.start()
    own_y.start()
    to_x = [send(hx_ref.at[xp(d)], hx.at[y, x], x_send.at[d - 1], x_recv.at[d - 1], at(y, xp(d), c, z))
            for d in range(1, NX)]
    to_y = [send(hy_ref.at[yp(d)], hy.at[y, x], y_send.at[d - 1], y_recv.at[d - 1], at(yp(d), x, c, z))
            for d in (1, 7, 2, 6, 3, 5, 4)]
    own_x.wait()
    for copy in to_x:
        copy.wait_recv()

    up, down = at(yp(1), x, c, z), at(yp(NY - 1), x, c, z)

    def ring(g, step):
        lanes = pl.ds(BASE[g], LANES[g])
        a, b = yp(NY - step), yp(step)
        if step < NY // 2 - 1:
            up_ref, down_ref = hx.at[a, :, :, lanes], hx.at[b, :, :, lanes]
        else:
            up_ref, down_ref = hx.at[a, 0:2, :, lanes], hx.at[b, 2:4, :, lanes]
        return (send(up_ref, up_ref, ring_send.at[0, g, step], ring_recv.at[0, g, step], up),
                send(down_ref, down_ref, ring_send.at[1, g, step], ring_recv.at[1, g, step], down))

    rings = {}
    rings[0, 0] = ring(0, 0)

    own_y.wait()
    for copy in to_y:
        copy.wait_recv()
    right, left = at(y, xp(1), c, z), at(y, xp(NX - 1), c, z)
    row0 = (send(hy.at[:, x], hy.at[:, x], row_send.at[0], row_recv.at[0], right),
            send(hy.at[:, x], hy.at[:, x], row_send.at[1], row_recv.at[1], left))

    for step in range(1, 4):
        for copy in rings[0, step - 1]:
            copy.wait_recv()
        rings[0, step] = ring(0, step)
        if step == 1:
            for copy in row0:
                copy.wait_recv()
            a, b = hy.at[0:4, xp(3)], hy.at[4:8, xp(1)]
            row1 = (send(a, a, row_send.at[2], row_recv.at[2], right),
                    send(b, b, row_send.at[3], row_recv.at[3], left))
    rings[1, 0] = ring(1, 0)
    for copy in row1:
        copy.wait_recv()
    for copy in rings[0, 3]:
        copy.wait_recv()

    minus, plus = at(y, x, c, zp(NZ - 1)), at(y, x, c, zp(1))
    sibling = at(y, x, 1 - c, z)
    result = []
    for g in range(2):
        size, lanes = GROUP[g], LANES[g]
        if g == 1:
            for copy in rings[1, 3]:
                copy.wait_recv()
        hy_all = hy[...].reshape(NY * NX * KP, YW)
        for j in range(0, lanes, TILE):
            hx_all = hx[:, :, :, BASE[g] + j:BASE[g] + j + TILE].reshape(NY * NX * KP, TILE)
            part[j:j + TILE, :] = lax.dot_general(
                hx_all, hy_all, (((0,), (0,)), ((), ())), preferred_element_type=jnp.float32)
        if g == 0:
            for copy in rings[1, 0]:
                copy.wait_recv()
            rings[1, 1] = ring(1, 1)
        mine = pl.ds(pl.multiple_of(c * YH, TILE), YH)
        other = pl.ds(pl.multiple_of((1 - c) * YH, TILE), YH)
        used = NZ * size
        sib_out[0:used, :] = part[0:used, other].astype(jnp.bfloat16)
        copy = send(sib_out.at[0:used], sib_in.at[g, 0:used], sib_send.at[g], sib_recv.at[g], sibling)
        copy.wait_recv()
        own[g, 0:used, :] = part[0:used, mine] + sib_in[g, 0:used, :].astype(jnp.float32)
        if g == 0:
            copy.wait_send()
            waits[:] = [w for w in waits if w is not copy]

        def piece(o, g=g, size=size):
            return own[g, pl.ds(pl.multiple_of(o * size, 16), size), :]

        before = None
        for step in range(6):
            now = []
            if before is not None:
                before[0].wait_recv()
            value = piece(zp(NZ - 6 + step))
            if before is not None:
                value = value + minus_in[g, step - 1, 0:size, :].astype(jnp.float32)
            minus_out[g, step, 0:size, :] = value.astype(jnp.bfloat16)
            now.append(send(minus_out.at[g, step, 0:size], minus_in.at[g, step, 0:size],
                            minus_send.at[g, step], minus_recv.at[g, step], minus))
            if step < 5:
                if before is not None:
                    before[1].wait_recv()
                value = piece(zp(5 - step))
                if before is not None:
                    value = value + plus_in[g, step - 1, 0:size, :].astype(jnp.float32)
                plus_out[g, step, 0:size, :] = value.astype(jnp.bfloat16)
                now.append(send(plus_out.at[g, step, 0:size], plus_in.at[g, step, 0:size],
                                plus_send.at[g, step], plus_recv.at[g, step], plus))
            elif before is not None:
                before[1].wait_recv()
            before = now
            if g == 0 and step in (1, 3):
                for copy in rings[1, 1 + step // 2]:
                    copy.wait_recv()
                rings[1, 2 + step // 2] = ring(1, 2 + step // 2)
        before[0].wait_recv()
        result.append(piece(z) + minus_in[g, 5, 0:size, :].astype(jnp.float32)
                      + plus_in[g, 4, 0:size, :].astype(jnp.float32))

    whole = jnp.concatenate(result, axis=0)
    for q in range(NX):
        final_out[q, :, 0:ROWS] = whole[:, q * ROWS:(q + 1) * ROWS]
        final_out[q, :, ROWS:TILE] = jnp.zeros((SEG, TILE - ROWS), jnp.float32)
    last = [send(final_out.at[xp(d)], final_in.at[x], fin_send.at[d - 1], fin_recv.at[d - 1], at(y, xp(d), c, z))
            for d in range(1, NX)]
    final_in[x] = final_out[x]
    for copy in last:
        copy.wait_recv()
    out_ref[...] = final_in[...].reshape(COLS, TILE).T[0:ROWS]
    for copy in waits:
        copy.wait_send()


def exchange(hx, hy):
    vmem = pl.BlockSpec(memory_space=pltpu.VMEM)
    dma = pltpu.SemaphoreType.DMA
    f32, bf16 = jnp.float32, jnp.bfloat16
    return pl.pallas_call(
        exchange_kernel,
        out_shape=jax.ShapeDtypeStruct((ROWS, COLS), f32),
        in_specs=[vmem, vmem],
        out_specs=vmem,
        scratch_shapes=[
            pltpu.VMEM((NY, NX, KP, XW), bf16),
            pltpu.VMEM((NY, NX, KP, YW), bf16),
            pltpu.VMEM((LANES[0], YW), f32),
            pltpu.VMEM((2, LANES[0], YH), f32),
            pltpu.VMEM((LANES[0], YH), bf16),
            pltpu.VMEM((2, LANES[0], YH), bf16),
            pltpu.VMEM((2, 6, GROUP[0], YH), bf16),
            pltpu.VMEM((2, 6, GROUP[0], YH), bf16),
            pltpu.VMEM((2, 5, GROUP[0], YH), bf16),
            pltpu.VMEM((2, 5, GROUP[0], YH), bf16),
            pltpu.VMEM((NX, SEG, TILE), f32),
            pltpu.VMEM((NX, SEG, TILE), f32),
            dma((2,)), dma((3,)), dma((3,)), dma((7,)), dma((7,)),
            dma((2, 2, 4)), dma((2, 2, 4)), dma((4,)), dma((4,)),
            dma((2,)), dma((2,)), dma((2, 6)), dma((2, 6)), dma((2, 5)), dma((2, 5)),
            dma((3,)), dma((3,)),
        ],
        compiler_params=pltpu.CompilerParams(
            collective_id=0, has_side_effects=True, vmem_limit_bytes=48 * 2**20),
    )(hx, hy)


def per_device(aux_tiles, orbitals, tile_rows, tile_cols, tile_count):
    hx, hy = half(aux_tiles, orbitals, tile_rows, tile_cols, tile_count)
    return exchange(hx, hy)


def solution(mesh):
    return jax.shard_map(
        per_device,
        mesh=mesh,
        in_specs=(
            P("aux", None, None, None),
            P("occ", None),
            P("aux", None),
            P("aux", None),
            P("aux"),
        ),
        out_specs=P("aux", "occ"),
        check_vma=False,
    )
```

```python
import functools

import jax
import jax.numpy as jnp
from jax import lax
from jax.experimental import pallas as pl
from jax.experimental.pallas import tpu as pltpu
from jax.sharding import PartitionSpec as P

MESH = pl.DeviceIdType.MESH
TILE = 128
NB = 42
NT = 64
PD = 4
OL = 4
BASIS = NB * TILE
NX, NY, NC, NZ = 4, 8, 2, 12
ROWS = 84
COLS = 448
SEG = COLS // NX
GROUP = (64, 48)
LANES = (768, 640)
BASE = (0, 768)
XW = 1408
YH = 384
YW = 2 * YH
KP = PD * OL
SLOTS_STEP = 8
GATHER = (
    (((0, 1, False), (0, 2, False)), ((2, 1, False), (2, 2, True))),
    (((0, 1, False),), ((1, 1, False),), ((2, 1, False), (2, 2, True))),
)
THREE = ((5, 4), (3, 2), (4, 2), (2, 0), (1, 0))
TWO = ((4, 3), (5, 3), (3, 0), (2, 0), (1, 0))
EDGES = ((THREE + ((6, 4),), THREE), (TWO + ((6, 3),), TWO))


def level(edges, node):
    return max((1 + level(edges, source) for source, target in edges if target == node), default=0)


def half_kernel(
    rows_hbm, cols_hbm, count_hbm, tiles_hbm, orb_hbm, hx_ref, hy_ref,
    rows_ref, cols_ref, count_ref, tiles, orb, acc, flat, sem, tile_sem,
):
    small = [
        pltpu.make_async_copy(rows_hbm, rows_ref, sem.at[0]),
        pltpu.make_async_copy(cols_hbm, cols_ref, sem.at[1]),
        pltpu.make_async_copy(count_hbm, count_ref, sem.at[2]),
        pltpu.make_async_copy(orb_hbm, orb, sem.at[3]),
    ]
    for copy in small:
        copy.start()
    big = []
    for k in range(NT // SLOTS_STEP):
        cut = pl.ds(k * SLOTS_STEP, SLOTS_STEP)
        big.append(pltpu.make_async_copy(tiles_hbm.at[:, cut], tiles.at[:, cut], tile_sem.at[k]))
        big[-1].start()
    acc[...] = jnp.zeros_like(acc)
    for copy in small:
        copy.wait()
    for k in range(NT // SLOTS_STEP):
        big[k].wait()
        for s in range(SLOTS_STEP):
            t = k * SLOTS_STEP + s
            row = rows_ref[0, t]
            col = cols_ref[0, t]
            block = orb[:, pl.ds(pl.multiple_of(col * TILE, TILE), TILE)]
            tile = tiles[:, t].reshape(PD * TILE, TILE)
            got = lax.dot_general(block, tile, (((1,), (1,)), ((), ())), preferred_element_type=jnp.float32)
            if t < NB:
                acc[row] += got
            else:
                acc[row] += jnp.where(t < count_ref[0], got, 0.0)
    for b in range(NB):
        for p in range(PD):
            flat[p * OL:(p + 1) * OL, b * TILE:(b + 1) * TILE] = acc[b, :, p * TILE:(p + 1) * TILE]
    for x in range(NX):
        parts = []
        for g in range(len(GROUP)):
            for o in range(NZ):
                a = o * COLS + x * SEG + sum(GROUP[:g])
                parts.append(flat[:, a:a + GROUP[g]])
            if LANES[g] > NZ * GROUP[g]:
                parts.append(jnp.zeros((KP, LANES[g] - NZ * GROUP[g]), jnp.float32))
        hx_ref[x] = jnp.concatenate(parts, axis=1).astype(jnp.bfloat16)
    for y in range(NY):
        parts = []
        for c in range(NC):
            for x in range(NX):
                a = ((y * NX + x) * NC + c) * ROWS
                parts.append(flat[:, a:a + ROWS])
            parts.append(jnp.zeros((KP, YH - NX * ROWS), jnp.float32))
        hy_ref[y] = jnp.concatenate(parts, axis=1).astype(jnp.bfloat16)


def half(aux_tiles, orbitals, tile_rows, tile_cols, tile_count):
    anywhere = pl.BlockSpec(memory_space=pl.ANY)
    vmem = pl.BlockSpec(memory_space=pltpu.VMEM)
    dma = pltpu.SemaphoreType.DMA
    return pl.pallas_call(
        half_kernel,
        in_specs=[anywhere] * 5,
        out_specs=[vmem] * 2,
        out_shape=[
            jax.ShapeDtypeStruct((NX, KP, XW), jnp.bfloat16),
            jax.ShapeDtypeStruct((NY, KP, YW), jnp.bfloat16),
        ],
        scratch_shapes=[
            pltpu.SMEM((1, NT), jnp.int32),
            pltpu.SMEM((1, NT), jnp.int32),
            pltpu.SMEM((1,), jnp.int32),
            pltpu.VMEM((PD, NT, TILE, TILE), jnp.bfloat16),
            pltpu.VMEM((OL, BASIS), jnp.bfloat16),
            pltpu.VMEM((NB, OL, PD * TILE), jnp.float32),
            pltpu.VMEM((KP, BASIS), jnp.float32),
            dma((4,)), dma((NT // SLOTS_STEP,)),
        ],
        compiler_params=pltpu.CompilerParams(vmem_limit_bytes=60 * 2**20),
    )(tile_rows, tile_cols, tile_count, aux_tiles, orbitals)


def exchange_kernel(
    hx_ref, hy_ref, out_ref,
    hx, hy, own, sib_out, sib_in, tree_out, tree_in, final_out, final_in,
    local_sem, x_send, x_recv, y_send, y_recv, ring_send, ring_recv, row_send, row_recv,
    sib_send, sib_recv, tree_send, tree_recv, fin_send, fin_recv,
):
    aux = lax.axis_index("aux")
    z = lax.axis_index("occ")
    c = lax.rem(aux, NC)
    x = lax.rem(aux // NC, NX)
    y = aux // (NC * NX)
    sign = 1 - 2 * c

    def at(y_, x_, c_, z_):
        return ((y_ * NX + x_) * NC + c_, z_)

    def xp(d):
        return lax.rem(x + d + NX, NX)

    def yp(d):
        return lax.rem(y + d + NY, NY)

    def zp(d):
        return lax.rem(z + sign * d + NZ, NZ)

    partners = [at(y, xp(d), c, z) for d in range(1, NX)]
    partners += [at(yp(d), x, c, z) for d in range(1, NY)]
    partners += [at(y, x, c, zp(d)) for d in (1, 2, 3, -1, -2, -3)]
    partners += [at(y, x, 1 - c, z)]
    barrier = pltpu.get_barrier_semaphore()
    for partner in partners:
        pl.semaphore_signal(barrier, inc=1, device_id=partner, device_id_type=MESH)
    pl.semaphore_wait(barrier, len(partners))

    started = []

    def send(src, dst, s_sem, r_sem, device):
        copy = pltpu.make_async_remote_copy(
            src_ref=src, dst_ref=dst, send_sem=s_sem, recv_sem=r_sem, device_id=device, device_id_type=MESH)
        copy.start()
        started.append(copy)
        return copy

    def arrive(copies):
        for copy in copies:
            copy.wait_recv()

    own_x = pltpu.make_async_copy(hx_ref.at[x], hx.at[y, x], local_sem.at[0])
    own_y = pltpu.make_async_copy(hy_ref.at[y], hy.at[y, x], local_sem.at[1])
    own_x.start()
    own_y.start()
    to_x = [send(hx_ref.at[xp(d)], hx.at[y, x], x_send.at[d - 1], x_recv.at[d - 1], at(y, xp(d), c, z))
            for d in range(1, NX)]
    to_y = [send(hy_ref.at[yp(d)], hy.at[y, x], y_send.at[d - 1], y_recv.at[d - 1], at(yp(d), x, c, z))
            for d in (1, 7, 2, 6, 3, 5, 4)]
    own_x.wait()
    arrive(to_x)

    rings = {}

    def ring(g, stage):
        lanes = pl.ds(BASE[g], LANES[g])
        count = sum(len(s) for s in GATHER[g][:stage])
        copies = []
        for n, (behind, hops, halved) in enumerate(GATHER[g][stage]):
            for way, turn in ((0, 1), (1, -1)):
                chunk = yp(-turn * behind)
                if halved:
                    ref = hx.at[chunk, 2 * way:2 * way + 2, :, lanes]
                else:
                    ref = hx.at[chunk, :, :, lanes]
                copies.append(send(ref, ref, ring_send.at[way, g, count + n], ring_recv.at[way, g, count + n],
                                   at(yp(turn * hops), x, c, z)))
        rings[g, stage] = copies

    ring(0, 0)
    ring(1, 0)

    own_y.wait()
    arrive(to_y)
    right, left = at(y, xp(1), c, z), at(y, xp(-1), c, z)
    row0 = (send(hy.at[:, x], hy.at[:, x], row_send.at[0], row_recv.at[0], right),
            send(hy.at[:, x], hy.at[:, x], row_send.at[1], row_recv.at[1], left))
    arrive(rings[0, 0])
    ring(0, 1)
    arrive(row0)
    a, b = hy.at[0:4, xp(-1)], hy.at[4:8, xp(1)]
    row1 = (send(a, a, row_send.at[2], row_recv.at[2], right),
            send(b, b, row_send.at[3], row_recv.at[3], left))
    arrive(rings[1, 0])
    ring(1, 1)
    arrive(row1)

    sibling = at(y, x, 1 - c, z)
    sib = {}

    def product(g, core, j):
        hx_all = hx[:, :, :, BASE[g] + j:BASE[g] + j + TILE].reshape(NY * NX * KP, TILE)
        hy_all = hy[:, :, :, pl.ds(pl.multiple_of(core * YH, TILE), YH)].reshape(NY * NX * KP, YH)
        return lax.dot_general(hx_all, hy_all, (((0,), (0,)), ((), ())), preferred_element_type=jnp.float32)

    def multiply(g):
        used = NZ * GROUP[g]
        for j in range(0, LANES[g], TILE):
            sib_out[g, j:j + TILE, :] = product(g, 1 - c, j).astype(jnp.bfloat16)
        sib[g] = send(sib_out.at[g, 0:used], sib_in.at[g, 0:used], sib_send.at[g], sib_recv.at[g], sibling)
        for j in range(0, LANES[g], TILE):
            own[g, j:j + TILE, :] = product(g, c, j)

    def add_sibling(g):
        used = NZ * GROUP[g]
        arrive([sib[g]])
        own[g, 0:used, :] += sib_in[g, 0:used, :].astype(jnp.float32)

    trees = {}

    def piece(g, o):
        return own[g, pl.ds(pl.multiple_of(o * GROUP[g], 16), GROUP[g]), :]

    def gathered(g, way, node, value):
        for n, (source, target) in enumerate(EDGES[g][way]):
            if target == node:
                arrive([trees[g, way, n]])
                value = value + tree_in[g, way, n, 0:GROUP[g], :].astype(jnp.float32)
        return value

    def tree(g, depth):
        for way, turn in ((0, 1), (1, -1)):
            edges = EDGES[g][way]
            for n, (source, target) in enumerate(edges):
                if level(edges, source) == depth:
                    value = gathered(g, way, source, piece(g, zp(-turn * source)))
                    tree_out[g, way, n, 0:GROUP[g], :] = value.astype(jnp.bfloat16)
                    trees[g, way, n] = send(
                        tree_out.at[g, way, n, 0:GROUP[g]], tree_in.at[g, way, n, 0:GROUP[g]],
                        tree_send.at[g, way, n], tree_recv.at[g, way, n], at(y, x, c, zp(-turn * (source - target))))

    arrive(rings[0, 1])
    multiply(0)
    arrive(rings[1, 1])
    ring(1, 2)
    add_sibling(0)
    tree(0, 0)
    arrive(rings[1, 2])
    multiply(1)
    tree(0, 1)
    add_sibling(1)
    tree(1, 0)
    tree(0, 2)
    tree(1, 1)
    result = []
    for g in range(2):
        value = piece(g, z)
        for way in range(2):
            value = gathered(g, way, 0, value)
        result.append(value)

    whole = jnp.concatenate(result, axis=0)
    for q in range(NX):
        final_out[q, :, 0:ROWS] = whole[:, q * ROWS:(q + 1) * ROWS]
        final_out[q, :, ROWS:TILE] = jnp.zeros((SEG, TILE - ROWS), jnp.float32)
    last = [send(final_out.at[xp(d)], final_in.at[x], fin_send.at[d - 1], fin_recv.at[d - 1], at(y, xp(d), c, z))
            for d in range(1, NX)]
    final_in[x] = final_out[x]
    arrive(last)
    out_ref[...] = final_in[...].reshape(COLS, TILE).T[0:ROWS]
    for copy in started:
        copy.wait_send()


def exchange(hx, hy):
    vmem = pl.BlockSpec(memory_space=pltpu.VMEM)
    dma = pltpu.SemaphoreType.DMA
    f32, bf16 = jnp.float32, jnp.bfloat16
    return pl.pallas_call(
        exchange_kernel,
        out_shape=jax.ShapeDtypeStruct((ROWS, COLS), f32),
        in_specs=[vmem, vmem],
        out_specs=vmem,
        scratch_shapes=[
            pltpu.VMEM((NY, NX, KP, XW), bf16),
            pltpu.VMEM((NY, NX, KP, YW), bf16),
            pltpu.VMEM((2, LANES[0], YH), f32),
            pltpu.VMEM((2, LANES[0], YH), bf16),
            pltpu.VMEM((2, LANES[0], YH), bf16),
            pltpu.VMEM((2, 2, 6, GROUP[0], YH), bf16),
            pltpu.VMEM((2, 2, 6, GROUP[0], YH), bf16),
            pltpu.VMEM((NX, SEG, TILE), f32),
            pltpu.VMEM((NX, SEG, TILE), f32),
            dma((2,)), dma((3,)), dma((3,)), dma((7,)), dma((7,)),
            dma((2, 2, 4)), dma((2, 2, 4)), dma((4,)), dma((4,)),
            dma((2,)), dma((2,)), dma((2, 2, 6)), dma((2, 2, 6)),
            dma((3,)), dma((3,)),
        ],
        compiler_params=pltpu.CompilerParams(
            collective_id=0, has_side_effects=True, vmem_limit_bytes=48 * 2**20),
    )(hx, hy)


def per_device(aux_tiles, orbitals, tile_rows, tile_cols, tile_count):
    hx, hy = half(aux_tiles, orbitals, tile_rows, tile_cols, tile_count)
    return exchange(hx, hy)


def solution(mesh):
    return jax.shard_map(
        per_device,
        mesh=mesh,
        in_specs=(
            P("aux", None, None, None),
            P("occ", None),
            P("aux", None),
            P("aux", None),
            P("aux"),
        ),
        out_specs=P("aux", "occ"),
        check_vma=False,
    )
```

```python
import functools

import jax
import jax.numpy as jnp
from jax import lax
from jax.experimental import pallas as pl
from jax.experimental.pallas import tpu as pltpu
from jax.sharding import PartitionSpec as P

MESH = pl.DeviceIdType.MESH
TILE = 128
NB = 42
NT = 64
PD = 4
OL = 4
BASIS = NB * TILE
NX, NY, NC, NZ = 4, 8, 2, 12
ROWS = 84
COLS = 448
SEG = COLS // NX
GROUP = (32, 48, 32)
LANES = tuple(-(-NZ * size // TILE) * TILE for size in GROUP)
BASE = tuple(sum(LANES[:g]) for g in range(len(GROUP)))
START = tuple(sum(GROUP[:g]) for g in range(len(GROUP)))
NG = len(GROUP)
XW = sum(LANES)
YH = 384
YW = 2 * YH
KP = PD * OL
NBP = 48
CUT = 8
AHEAD = 3
QUICK = (((0, 1, False), (0, 2, False)), ((2, 1, False), (2, 2, True)))
LIGHT = (((0, 1, False),), ((1, 1, False),), ((2, 1, False), (2, 2, True)))
GATHER = (LIGHT, LIGHT, LIGHT)
THREE = ((5, 4), (3, 2), (4, 2), (2, 0), (1, 0))
TWO = ((4, 3), (5, 3), (3, 0), (2, 0), (1, 0))
EDGES = ((THREE + ((6, 4),), THREE),) * NG


def level(edges, node):
    return max((1 + level(edges, source) for source, target in edges if target == node), default=0)


def fetch(tiles_hbm, tiles, tile_sem, k):
    cut = pl.ds(k * CUT, CUT)
    return pltpu.make_async_copy(tiles_hbm.at[:, cut], tiles.at[:, cut], tile_sem.at[k])


def half(rows_v, cols_v, count_s, tiles_hbm, tiles, orb, by_block, chosen, tile_sem, copies, slots, placed, flat,
         hx_own, hy_own):
    for copy in copies:
        copy.wait()
    block_id = lax.broadcasted_iota(jnp.int32, (NBP, NT), 0)
    slot_id = lax.broadcasted_iota(jnp.int32, (NBP, NT), 1)
    by_block[...] = jnp.zeros_like(by_block)
    for b in range(NB):
        by_block[:, b, :] = orb[:, b * TILE:(b + 1) * TILE].astype(jnp.float32)
    hot = jnp.where(cols_v[...] == block_id, 1.0, 0.0).astype(jnp.bfloat16)
    for i in range(OL):
        chosen[i] = lax.dot_general(hot, by_block[i].astype(jnp.bfloat16), (((0,), (0,)), ((), ())),
                                    preferred_element_type=jnp.float32)
    for k in range(NT // CUT):
        fetch(tiles_hbm, tiles, tile_sem, k).wait()
        if k + AHEAD < NT // CUT:
            fetch(tiles_hbm, tiles, tile_sem, k + AHEAD).start()
        for t in range(k * CUT, (k + 1) * CUT):
            block = chosen[:, t, :].astype(jnp.bfloat16)
            tile = tiles[:, t].reshape(PD * TILE, TILE)
            got = lax.dot_general(block, tile, (((1,), (1,)), ((), ())), preferred_element_type=jnp.float32)
            for p in range(PD):
                slots[p * OL:(p + 1) * OL, t, :] = got[:, p * TILE:(p + 1) * TILE]
    hot = jnp.where((rows_v[...] == block_id) & (slot_id < count_s[0]), 1.0, 0.0).astype(jnp.bfloat16)
    hot = jnp.concatenate([hot, hot, hot], axis=1)
    for k in range(0, KP, 2):
        parts = []
        for j in (k, k + 1):
            value = slots[j]
            high = value.astype(jnp.bfloat16)
            rest = value - high.astype(jnp.float32)
            middle = rest.astype(jnp.bfloat16)
            low = (rest - middle.astype(jnp.float32)).astype(jnp.bfloat16)
            parts.append(jnp.concatenate([high, middle, low], axis=0))
        sums = jnp.dot(hot, jnp.concatenate(parts, axis=1), preferred_element_type=jnp.float32)
        placed[k] = sums[:, 0:TILE]
        placed[k + 1] = sums[:, TILE:2 * TILE]
    for b in range(NB):
        flat[:, b * TILE:(b + 1) * TILE] = placed[:, b, :]
    for x in range(NX):
        parts = []
        for g in range(NG):
            for o in range(NZ):
                a = o * COLS + x * SEG + START[g]
                parts.append(flat[:, a:a + GROUP[g]])
            if LANES[g] > NZ * GROUP[g]:
                parts.append(jnp.zeros((KP, LANES[g] - NZ * GROUP[g]), jnp.float32))
        hx_own[x] = jnp.concatenate(parts, axis=1).astype(jnp.bfloat16)
    for y in range(NY):
        parts = []
        for c in range(NC):
            for x in range(NX):
                a = ((y * NX + x) * NC + c) * ROWS
                parts.append(flat[:, a:a + ROWS])
            parts.append(jnp.zeros((KP, YH - NX * ROWS), jnp.float32))
        hy_own[y] = jnp.concatenate(parts, axis=1).astype(jnp.bfloat16)


def exchange_kernel(
    rows_hbm, cols_hbm, count_hbm, tiles_hbm, orb_hbm, out_ref,
    rows_v, cols_v, count_s, tiles, orb, by_block, chosen, slots, placed, flat, hx_ref, hy_ref,
    hx, hy, own, sib_out, sib_in, tree_out, tree_in, final_out, final_in,
    local_sem, tile_sem, x_send, x_recv, y_send, y_recv, ring_send, ring_recv, row_send, row_recv,
    sib_send, sib_recv, tree_send, tree_recv, fin_send, fin_recv,
):
    aux = lax.axis_index("aux")
    z = lax.axis_index("occ")
    c = lax.rem(aux, NC)
    x = lax.rem(aux // NC, NX)
    y = aux // (NC * NX)
    sign = 1 - 2 * c

    def at(y_, x_, c_, z_):
        return ((y_ * NX + x_) * NC + c_, z_)

    def xp(d):
        return lax.rem(x + d + NX, NX)

    def yp(d):
        return lax.rem(y + d + NY, NY)

    def zp(d):
        return lax.rem(z + sign * d + NZ, NZ)

    small = [
        pltpu.make_async_copy(rows_hbm, rows_v, local_sem.at[0]),
        pltpu.make_async_copy(cols_hbm, cols_v, local_sem.at[1]),
        pltpu.make_async_copy(count_hbm, count_s, local_sem.at[2]),
        pltpu.make_async_copy(orb_hbm, orb, local_sem.at[3]),
    ]
    for copy in small:
        copy.start()
    for k in range(AHEAD):
        fetch(tiles_hbm, tiles, tile_sem, k).start()
    partners = [at(y, xp(d), c, z) for d in range(1, NX)]
    partners += [at(yp(d), x, c, z) for d in range(1, NY)]
    partners += [at(y, x, c, zp(d)) for d in (1, 2, 3, -1, -2, -3)]
    partners += [at(y, x, 1 - c, z)]
    barrier = pltpu.get_barrier_semaphore()
    for partner in partners:
        pl.semaphore_signal(barrier, inc=1, device_id=partner, device_id_type=MESH)
    half(rows_v, cols_v, count_s, tiles_hbm, tiles, orb, by_block, chosen, tile_sem, small, slots, placed, flat, hx_ref, hy_ref)
    pl.semaphore_wait(barrier, len(partners))

    started = []

    def send(src, dst, s_sem, r_sem, device):
        copy = pltpu.make_async_remote_copy(
            src_ref=src, dst_ref=dst, send_sem=s_sem, recv_sem=r_sem, device_id=device, device_id_type=MESH)
        copy.start()
        started.append(copy)
        return copy

    def arrive(copies):
        for copy in copies:
            copy.wait_recv()

    to_x = [send(hx_ref.at[xp(d)], hx.at[y, x], x_send.at[d - 1], x_recv.at[d - 1], at(y, xp(d), c, z))
            for d in range(1, NX)]
    order = (1, 7, 2, 6, 3, 5, 4)
    to_y = {d: send(hy_ref.at[yp(d)], hy.at[y, x], y_send.at[d - 1], y_recv.at[d - 1], at(yp(d), x, c, z))
            for d in order}
    hx[y, x] = hx_ref[x]
    hy[y, x] = hy_ref[y]

    right, left = at(y, xp(1), c, z), at(y, xp(-1), c, z)
    row0, row1 = {}, {}

    def spread(d):
        piece_ref = hy.at[yp(-d), x]
        row0[d] = (send(piece_ref, piece_ref, row_send.at[0, d], row_recv.at[0, d], right),
                   send(piece_ref, piece_ref, row_send.at[1, d], row_recv.at[1, d], left))

    def pass_on(d):
        arrive(row0[d])
        way = d % 2
        piece_ref = hy.at[yp(-d), xp(1 if way else -1)]
        row1[d] = send(piece_ref, piece_ref, row_send.at[2, d], row_recv.at[2, d], left if way else right)

    spread(0)
    arrive(to_x)

    rings = {}

    def ring(g, stage):
        lanes = pl.ds(BASE[g], LANES[g])
        count = sum(len(s) for s in GATHER[g][:stage])
        copies = []
        for n, (behind, hops, halved) in enumerate(GATHER[g][stage]):
            for way, turn in ((0, 1), (1, -1)):
                chunk = yp(-turn * behind)
                if halved:
                    ref = hx.at[chunk, 2 * way:2 * way + 2, :, lanes]
                else:
                    ref = hx.at[chunk, :, :, lanes]
                copies.append(send(ref, ref, ring_send.at[way, g, count + n], ring_recv.at[way, g, count + n],
                                   at(yp(turn * hops), x, c, z)))
        rings[g, stage] = copies

    for g in range(NG):
        ring(g, 0)
    for d in order:
        arrive([to_y[d]])
        spread(d)
    arrive(rings[0, 0])
    ring(0, 1)
    for d in (0,) + order[:3]:
        pass_on(d)
    for g in range(1, NG):
        arrive(rings[g, 0])
        ring(g, 1)
    for d in order[3:]:
        pass_on(d)
    for g in range(NG):
        if len(GATHER[g]) > 2:
            arrive(rings[g, 1])
            ring(g, 2)
    arrive(row1.values())

    sibling = at(y, x, 1 - c, z)
    sib = {}

    def product(g, core, j):
        hx_all = hx[:, :, :, BASE[g] + j:BASE[g] + j + TILE].reshape(NY * NX * KP, TILE)
        hy_all = hy[:, :, :, pl.ds(pl.multiple_of(core * YH, TILE), YH)].reshape(NY * NX * KP, YH)
        return lax.dot_general(hx_all, hy_all, (((0,), (0,)), ((), ())), preferred_element_type=jnp.float32)

    def multiply(g):
        used = NZ * GROUP[g]
        for j in range(0, LANES[g], TILE):
            sib_out[g, j:j + TILE, :] = product(g, 1 - c, j).astype(jnp.bfloat16)
        sib[g] = send(sib_out.at[g, 0:used], sib_in.at[g, 0:used], sib_send.at[g], sib_recv.at[g], sibling)
        for j in range(0, LANES[g], TILE):
            own[g, j:j + TILE, :] = product(g, c, j)

    def add_sibling(g):
        used = NZ * GROUP[g]
        sib[g].wait_recv()
        own[g, 0:used, :] += sib_in[g, 0:used, :].astype(jnp.float32)

    trees = {}

    def piece(g, o):
        return own[g, pl.ds(pl.multiple_of(o * GROUP[g], 16), GROUP[g]), :]

    def gathered(g, way, node, value):
        for n, (source, target) in enumerate(EDGES[g][way]):
            if target == node:
                trees[g, way, n].wait_recv()
                value = value + tree_in[g, way, n, 0:GROUP[g], :].astype(jnp.float32)
        return value

    def tree(g, depth):
        for way, turn in ((0, 1), (1, -1)):
            edges = EDGES[g][way]
            for n, (source, target) in enumerate(edges):
                if level(edges, source) == depth:
                    value = gathered(g, way, source, piece(g, zp(-turn * source)))
                    tree_out[g, way, n, 0:GROUP[g], :] = value.astype(jnp.bfloat16)
                    trees[g, way, n] = send(
                        tree_out.at[g, way, n, 0:GROUP[g]], tree_in.at[g, way, n, 0:GROUP[g]],
                        tree_send.at[g, way, n], tree_recv.at[g, way, n], at(y, x, c, zp(-turn * (source - target))))

    for g in range(NG):
        arrive(rings[g, len(GATHER[g]) - 1])
        multiply(g)
        add_sibling(g)
        tree(g, 0)
    for depth in (1, 2):
        for g in range(NG):
            tree(g, depth)
    last = []
    for g in range(NG):
        value = piece(g, z)
        for way in range(2):
            value = gathered(g, way, 0, value)
        rows = pl.ds(START[g], GROUP[g])
        for q in range(NX):
            final_out[q, rows, 0:ROWS] = value[:, q * ROWS:(q + 1) * ROWS]
            final_out[q, rows, ROWS:TILE] = jnp.zeros((GROUP[g], TILE - ROWS), jnp.float32)
        last += [send(final_out.at[xp(d), rows], final_in.at[x, rows], fin_send.at[g, d - 1], fin_recv.at[g, d - 1],
                      at(y, xp(d), c, z)) for d in range(1, NX)]
        final_in[x, rows] = final_out[x, rows]
    arrive(last)
    out_ref[...] = final_in[...].reshape(COLS, TILE).T[0:ROWS]
    for copy in started:
        copy.wait_send()


def per_device(aux_tiles, orbitals, tile_rows, tile_cols, tile_count):
    anywhere = pl.BlockSpec(memory_space=pl.ANY)
    dma = pltpu.SemaphoreType.DMA
    f32, bf16 = jnp.float32, jnp.bfloat16
    most = max(LANES)
    return pl.pallas_call(
        exchange_kernel,
        out_shape=jax.ShapeDtypeStruct((ROWS, COLS), f32),
        in_specs=[anywhere] * 5,
        out_specs=pl.BlockSpec(memory_space=pltpu.VMEM),
        scratch_shapes=[
            pltpu.VMEM((1, NT), jnp.int32),
            pltpu.VMEM((1, NT), jnp.int32),
            pltpu.SMEM((1,), jnp.int32),
            pltpu.VMEM((PD, NT, TILE, TILE), bf16),
            pltpu.VMEM((OL, BASIS), bf16),
            pltpu.VMEM((OL, NBP, TILE), f32),
            pltpu.VMEM((OL, NT, TILE), f32),
            pltpu.VMEM((KP, NT, TILE), f32),
            pltpu.VMEM((KP, NBP, TILE), f32),
            pltpu.VMEM((KP, BASIS), f32),
            pltpu.VMEM((NX, KP, XW), bf16),
            pltpu.VMEM((NY, KP, YW), bf16),
            pltpu.VMEM((NY, NX, KP, XW), bf16),
            pltpu.VMEM((NY, NX, KP, YW), bf16),
            pltpu.VMEM((NG, most, YH), f32),
            pltpu.VMEM((NG, most, YH), bf16),
            pltpu.VMEM((NG, most, YH), bf16),
            pltpu.VMEM((NG, 2, 6, max(GROUP), YH), bf16),
            pltpu.VMEM((NG, 2, 6, max(GROUP), YH), bf16),
            pltpu.VMEM((NX, SEG, TILE), f32),
            pltpu.VMEM((NX, SEG, TILE), f32),
            dma((4,)), dma((NT // CUT,)), dma((3,)), dma((3,)), dma((7,)), dma((7,)),
            dma((2, NG, 4)), dma((2, NG, 4)), dma((3, NY)), dma((3, NY)),
            dma((NG,)), dma((NG,)), dma((NG, 2, 6)), dma((NG, 2, 6)),
            dma((NG, 3)), dma((NG, 3)),
        ],
        compiler_params=pltpu.CompilerParams(
            collective_id=0, has_side_effects=True, vmem_limit_bytes=56 * 2**20),
    )(tile_rows, tile_cols, tile_count, aux_tiles, orbitals)


def solution(mesh):
    return jax.shard_map(
        per_device,
        mesh=mesh,
        in_specs=(
            P("aux", None, None, None),
            P("occ", None),
            P("aux", None),
            P("aux", None),
            P("aux"),
        ),
        out_specs=P("aux", "occ"),
        check_vma=False,
    )
```

```python
import functools

import jax
import jax.numpy as jnp
from jax import lax
from jax.experimental import pallas as pl
from jax.experimental.pallas import tpu as pltpu
from jax.sharding import PartitionSpec as P

MESH = pl.DeviceIdType.MESH
TILE = 128
NB = 42
NT = 64
PD = 4
OL = 4
BASIS = NB * TILE
NX, NY, NC, NZ = 4, 8, 2, 12
ROWS = 84
COLS = 448
SEG = COLS // NX
GROUP = (32, 32, 32, 16)
LANES = tuple(-(-NZ * size // TILE) * TILE for size in GROUP)
BASE = tuple(sum(LANES[:g]) for g in range(len(GROUP)))
START = tuple(sum(GROUP[:g]) for g in range(len(GROUP)))
NG = len(GROUP)
XW = sum(LANES)
YH = 384
YW = 2 * YH
KP = PD * OL
NBP = 48
CUT = 8
AHEAD = 3
QUICK = (((0, 1, False), (0, 2, False)), ((2, 1, False), (2, 2, True)))
LIGHT = (((0, 1, False),), ((1, 1, False),), ((2, 1, False), (2, 2, True)))
GATHER = (LIGHT,) * NG
THREE = ((5, 4), (3, 2), (1, 0), (4, 2), (2, 0))
TWO = ((4, 3), (5, 3), (3, 0), (2, 0), (1, 0))
EDGES = ((((6, 4),) + THREE, THREE),) * NG


def level(edges, node):
    return max((1 + level(edges, source) for source, target in edges if target == node), default=0)


def fetch(tiles_hbm, tiles, tile_sem, k):
    cut = pl.ds(k * CUT, CUT)
    return pltpu.make_async_copy(tiles_hbm.at[:, cut], tiles.at[:, cut], tile_sem.at[k])


def half(rows_v, cols_v, count_s, tiles_hbm, tiles, orb, by_block, chosen, tile_sem, copies, slots, placed, flat,
         hx_own, hy_own):
    for copy in copies:
        copy.wait()
    block_id = lax.broadcasted_iota(jnp.int32, (NBP, NT), 0)
    slot_id = lax.broadcasted_iota(jnp.int32, (NBP, NT), 1)
    by_block[...] = jnp.zeros_like(by_block)
    for b in range(NB):
        by_block[:, b, :] = orb[:, b * TILE:(b + 1) * TILE].astype(jnp.float32)
    hot = jnp.where(cols_v[...] == block_id, 1.0, 0.0).astype(jnp.bfloat16)
    for i in range(OL):
        chosen[i] = lax.dot_general(hot, by_block[i].astype(jnp.bfloat16), (((0,), (0,)), ((), ())),
                                    preferred_element_type=jnp.float32)
    for k in range(NT // CUT):
        fetch(tiles_hbm, tiles, tile_sem, k).wait()
        if k + AHEAD < NT // CUT:
            fetch(tiles_hbm, tiles, tile_sem, k + AHEAD).start()
        for t in range(k * CUT, (k + 1) * CUT):
            block = chosen[:, t, :].astype(jnp.bfloat16)
            tile = tiles[:, t].reshape(PD * TILE, TILE)
            got = lax.dot_general(block, tile, (((1,), (1,)), ((), ())), preferred_element_type=jnp.float32)
            for p in range(PD):
                slots[p * OL:(p + 1) * OL, t, :] = got[:, p * TILE:(p + 1) * TILE]
    hot = jnp.where((rows_v[...] == block_id) & (slot_id < count_s[0]), 1.0, 0.0).astype(jnp.bfloat16)
    hot = jnp.concatenate([hot, hot, hot], axis=1)
    for k in range(0, KP, 2):
        parts = []
        for j in (k, k + 1):
            value = slots[j]
            high = value.astype(jnp.bfloat16)
            rest = value - high.astype(jnp.float32)
            middle = rest.astype(jnp.bfloat16)
            low = (rest - middle.astype(jnp.float32)).astype(jnp.bfloat16)
            parts.append(jnp.concatenate([high, middle, low], axis=0))
        sums = jnp.dot(hot, jnp.concatenate(parts, axis=1), preferred_element_type=jnp.float32)
        placed[k] = sums[:, 0:TILE]
        placed[k + 1] = sums[:, TILE:2 * TILE]
    for b in range(NB):
        flat[:, b * TILE:(b + 1) * TILE] = placed[:, b, :]
    for x in range(NX):
        parts = []
        for g in range(NG):
            for o in range(NZ):
                a = o * COLS + x * SEG + START[g]
                parts.append(flat[:, a:a + GROUP[g]])
            if LANES[g] > NZ * GROUP[g]:
                parts.append(jnp.zeros((KP, LANES[g] - NZ * GROUP[g]), jnp.float32))
        hx_own[x] = jnp.concatenate(parts, axis=1).astype(jnp.bfloat16)
    for y in range(NY):
        parts = []
        for c in range(NC):
            for x in range(NX):
                a = ((y * NX + x) * NC + c) * ROWS
                parts.append(flat[:, a:a + ROWS])
            parts.append(jnp.zeros((KP, YH - NX * ROWS), jnp.float32))
        hy_own[y] = jnp.concatenate(parts, axis=1).astype(jnp.bfloat16)


def exchange_kernel(
    rows_hbm, cols_hbm, count_hbm, tiles_hbm, orb_hbm, out_ref,
    rows_v, cols_v, count_s, tiles, orb, by_block, chosen, slots, placed, flat, hx_ref, hy_ref,
    hx, hy, own, sib_out, sib_in, tree_out, tree_in, final_out, final_in,
    local_sem, tile_sem, x_send, x_recv, y_send, y_recv, ring_send, ring_recv, row_send, row_recv,
    sib_send, sib_recv, tree_send, tree_recv, fin_send, fin_recv,
):
    aux = lax.axis_index("aux")
    z = lax.axis_index("occ")
    c = lax.rem(aux, NC)
    x = lax.rem(aux // NC, NX)
    y = aux // (NC * NX)
    sign = 1 - 2 * c

    def at(y_, x_, c_, z_):
        return ((y_ * NX + x_) * NC + c_, z_)

    def xp(d):
        return lax.rem(x + d + NX, NX)

    def yp(d):
        return lax.rem(y + d + NY, NY)

    def zp(d):
        return lax.rem(z + sign * d + NZ, NZ)

    small = [
        pltpu.make_async_copy(rows_hbm, rows_v, local_sem.at[0]),
        pltpu.make_async_copy(cols_hbm, cols_v, local_sem.at[1]),
        pltpu.make_async_copy(count_hbm, count_s, local_sem.at[2]),
        pltpu.make_async_copy(orb_hbm, orb, local_sem.at[3]),
    ]
    for copy in small:
        copy.start()
    for k in range(AHEAD):
        fetch(tiles_hbm, tiles, tile_sem, k).start()
    partners = [at(y, xp(d), c, z) for d in range(1, NX)]
    partners += [at(yp(d), x, c, z) for d in range(1, NY)]
    partners += [at(y, x, c, zp(d)) for d in (1, 2, 3, -1, -2, -3)]
    partners += [at(y, x, 1 - c, z)]
    barrier = pltpu.get_barrier_semaphore()
    for partner in partners:
        pl.semaphore_signal(barrier, inc=1, device_id=partner, device_id_type=MESH)
    half(rows_v, cols_v, count_s, tiles_hbm, tiles, orb, by_block, chosen, tile_sem, small, slots, placed, flat, hx_ref, hy_ref)
    pl.semaphore_wait(barrier, len(partners))

    started = []

    def send(src, dst, s_sem, r_sem, device):
        copy = pltpu.make_async_remote_copy(
            src_ref=src, dst_ref=dst, send_sem=s_sem, recv_sem=r_sem, device_id=device, device_id_type=MESH)
        copy.start()
        started.append(copy)
        return copy

    def arrive(copies):
        for copy in copies:
            copy.wait_recv()

    def hand_out(part, lanes):
        return [send(hx_ref.at[xp(d), :, lanes], hx.at[y, x, :, lanes], x_send.at[part, d - 1], x_recv.at[part, d - 1],
                     at(y, xp(d), c, z)) for d in (1, 3, 2)]

    to_x = [hand_out(0, pl.ds(0, LANES[0])), hand_out(1, pl.ds(LANES[0], XW - LANES[0]))]
    order = (1, 7, 2, 6, 3, 5, 4)
    to_y = {d: send(hy_ref.at[yp(d)], hy.at[y, x], y_send.at[d - 1], y_recv.at[d - 1], at(yp(d), x, c, z))
            for d in order}
    hx[y, x] = hx_ref[x]
    hy[y, x] = hy_ref[y]

    right, left = at(y, xp(1), c, z), at(y, xp(-1), c, z)
    row0, row1 = {}, {}

    def spread(d):
        piece_ref = hy.at[yp(-d), x]
        row0[d] = (send(piece_ref, piece_ref, row_send.at[0, d], row_recv.at[0, d], right),
                   send(piece_ref, piece_ref, row_send.at[1, d], row_recv.at[1, d], left))

    def pass_on(d):
        arrive(row0[d])
        way = d % 2
        piece_ref = hy.at[yp(-d), xp(1 if way else -1)]
        row1[d] = send(piece_ref, piece_ref, row_send.at[2, d], row_recv.at[2, d], left if way else right)

    spread(0)

    rings = {}

    def ring(g, stage):
        lanes = pl.ds(BASE[g], LANES[g])
        count = sum(len(s) for s in GATHER[g][:stage])
        copies = []
        for n, (behind, hops, halved) in enumerate(GATHER[g][stage]):
            for way, turn in ((0, 1), (1, -1)):
                chunk = yp(-turn * behind)
                if halved:
                    ref = hx.at[chunk, 2 * way:2 * way + 2, :, lanes]
                else:
                    ref = hx.at[chunk, :, :, lanes]
                copies.append(send(ref, ref, ring_send.at[way, g, count + n], ring_recv.at[way, g, count + n],
                                   at(yp(turn * hops), x, c, z)))
        rings[g, stage] = copies

    arrive(to_x[0])
    ring(0, 0)
    arrive(to_x[1])
    for g in range(1, NG):
        ring(g, 0)
    for d in order:
        arrive([to_y[d]])
        spread(d)
    arrive(rings[0, 0])
    ring(0, 1)
    for d in (0,) + order[:3]:
        pass_on(d)
    for g in range(1, NG):
        arrive(rings[g, 0])
        ring(g, 1)
    for d in order[3:]:
        pass_on(d)
    for g in range(NG):
        if len(GATHER[g]) > 2:
            arrive(rings[g, 1])
            ring(g, 2)
    arrive(row1.values())

    sibling = at(y, x, 1 - c, z)
    sib = {}

    def product(g, core, j):
        hx_all = hx[:, :, :, BASE[g] + j:BASE[g] + j + TILE].reshape(NY * NX * KP, TILE)
        hy_all = hy[:, :, :, pl.ds(pl.multiple_of(core * YH, TILE), YH)].reshape(NY * NX * KP, YH)
        return lax.dot_general(hx_all, hy_all, (((0,), (0,)), ((), ())), preferred_element_type=jnp.float32)

    def multiply(g):
        used = NZ * GROUP[g]
        for j in range(0, LANES[g], TILE):
            sib_out[g, j:j + TILE, :] = product(g, 1 - c, j).astype(jnp.bfloat16)
        sib[g] = send(sib_out.at[g, 0:used], sib_in.at[g, 0:used], sib_send.at[g], sib_recv.at[g], sibling)
        for j in range(0, LANES[g], TILE):
            own[g, j:j + TILE, :] = product(g, c, j)

    def add_sibling(g):
        used = NZ * GROUP[g]
        sib[g].wait_recv()
        own[g, 0:used, :] += sib_in[g, 0:used, :].astype(jnp.float32)

    trees = {}

    def piece(g, o):
        return own[g, pl.ds(pl.multiple_of(o * GROUP[g], 16), GROUP[g]), :]

    def gathered(g, way, node, value):
        for n, (source, target) in enumerate(EDGES[g][way]):
            if target == node:
                trees[g, way, n].wait_recv()
                value = value + tree_in[g, way, n, 0:GROUP[g], :].astype(jnp.float32)
        return value

    def tree(g, depth):
        for n in range(6):
            for way, turn in ((0, 1), (1, -1)):
                edges = EDGES[g][way]
                if n < len(edges) and level(edges, edges[n][0]) == depth:
                    source, target = edges[n]
                    value = gathered(g, way, source, piece(g, zp(-turn * source)))
                    tree_out[g, way, n, 0:GROUP[g], :] = value.astype(jnp.bfloat16)
                    trees[g, way, n] = send(
                        tree_out.at[g, way, n, 0:GROUP[g]], tree_in.at[g, way, n, 0:GROUP[g]],
                        tree_send.at[g, way, n], tree_recv.at[g, way, n], at(y, x, c, zp(-turn * (source - target))))

    for g in range(NG):
        arrive(rings[g, len(GATHER[g]) - 1])
        multiply(g)
        if g == NG - 2:
            continue
        if g == NG - 1:
            add_sibling(g - 1)
            tree(g - 1, 0)
        add_sibling(g)
        tree(g, 0)
    for depth in (1, 2):
        for g in range(NG):
            tree(g, depth)
    last = []
    for g in range(NG):
        value = piece(g, z)
        for way in range(2):
            value = gathered(g, way, 0, value)
        rows = pl.ds(START[g], GROUP[g])
        for q in range(NX):
            final_out[q, rows, 0:ROWS] = value[:, q * ROWS:(q + 1) * ROWS]
            final_out[q, rows, ROWS:TILE] = jnp.zeros((GROUP[g], TILE - ROWS), jnp.float32)
        last += [send(final_out.at[xp(d), rows], final_in.at[x, rows], fin_send.at[g, d - 1], fin_recv.at[g, d - 1],
                      at(y, xp(d), c, z)) for d in range(1, NX)]
        final_in[x, rows] = final_out[x, rows]
    arrive(last)
    out_ref[...] = final_in[...].reshape(COLS, TILE).T[0:ROWS]
    for copy in started:
        copy.wait_send()


def per_device(aux_tiles, orbitals, tile_rows, tile_cols, tile_count):
    anywhere = pl.BlockSpec(memory_space=pl.ANY)
    dma = pltpu.SemaphoreType.DMA
    f32, bf16 = jnp.float32, jnp.bfloat16
    most = max(LANES)
    return pl.pallas_call(
        exchange_kernel,
        out_shape=jax.ShapeDtypeStruct((ROWS, COLS), f32),
        in_specs=[anywhere] * 5,
        out_specs=pl.BlockSpec(memory_space=pltpu.VMEM),
        scratch_shapes=[
            pltpu.VMEM((1, NT), jnp.int32),
            pltpu.VMEM((1, NT), jnp.int32),
            pltpu.SMEM((1,), jnp.int32),
            pltpu.VMEM((PD, NT, TILE, TILE), bf16),
            pltpu.VMEM((OL, BASIS), bf16),
            pltpu.VMEM((OL, NBP, TILE), f32),
            pltpu.VMEM((OL, NT, TILE), f32),
            pltpu.VMEM((KP, NT, TILE), f32),
            pltpu.VMEM((KP, NBP, TILE), f32),
            pltpu.VMEM((KP, BASIS), f32),
            pltpu.VMEM((NX, KP, XW), bf16),
            pltpu.VMEM((NY, KP, YW), bf16),
            pltpu.VMEM((NY, NX, KP, XW), bf16),
            pltpu.VMEM((NY, NX, KP, YW), bf16),
            pltpu.VMEM((NG, most, YH), f32),
            pltpu.VMEM((NG, most, YH), bf16),
            pltpu.VMEM((NG, most, YH), bf16),
            pltpu.VMEM((NG, 2, 6, max(GROUP), YH), bf16),
            pltpu.VMEM((NG, 2, 6, max(GROUP), YH), bf16),
            pltpu.VMEM((NX, SEG, TILE), f32),
            pltpu.VMEM((NX, SEG, TILE), f32),
            dma((4,)), dma((NT // CUT,)), dma((2, 3)), dma((2, 3)), dma((7,)), dma((7,)),
            dma((2, NG, 4)), dma((2, NG, 4)), dma((3, NY)), dma((3, NY)),
            dma((NG,)), dma((NG,)), dma((NG, 2, 6)), dma((NG, 2, 6)),
            dma((NG, 3)), dma((NG, 3)),
        ],
        compiler_params=pltpu.CompilerParams(
            collective_id=0, has_side_effects=True, vmem_limit_bytes=56 * 2**20),
    )(tile_rows, tile_cols, tile_count, aux_tiles, orbitals)


def solution(mesh):
    return jax.shard_map(
        per_device,
        mesh=mesh,
        in_specs=(
            P("aux", None, None, None),
            P("occ", None),
            P("aux", None),
            P("aux", None),
            P("aux"),
        ),
        out_specs=P("aux", "occ"),
        check_vma=False,
    )
```

```python
import functools

import jax
import jax.numpy as jnp
from jax import lax
from jax.experimental import pallas as pl
from jax.experimental.pallas import tpu as pltpu
from jax.sharding import PartitionSpec as P

MESH = pl.DeviceIdType.MESH
TILE = 128
NB = 42
NT = 64
PD = 4
OL = 4
BASIS = NB * TILE
NX, NY, NC, NZ = 4, 8, 2, 12
ROWS = 84
COLS = 448
SEG = COLS // NX
GROUP = (32, 32, 32, 16)
LANES = tuple(-(-NZ * size // TILE) * TILE for size in GROUP)
BASE = tuple(sum(LANES[:g]) for g in range(len(GROUP)))
START = tuple(sum(GROUP[:g]) for g in range(len(GROUP)))
NG = len(GROUP)
XW = sum(LANES)
YH = 384
YW = 2 * YH
KP = PD * OL
NBP = 48
CUT = 16
AHEAD = 2
QUICK = (((0, 1, False), (0, 2, False)), ((2, 1, False), (2, 2, True)))
LIGHT = (((0, 1, False),), ((1, 1, False),), ((2, 1, False), (2, 2, True)))
GATHER = (LIGHT,) * NG
THREE = ((5, 4), (3, 2), (1, 0), (4, 2), (2, 0))
TWO = ((4, 3), (5, 3), (3, 0), (2, 0), (1, 0))
EDGES = ((((6, 4),) + THREE, THREE),) * NG


def level(edges, node):
    return max((1 + level(edges, source) for source, target in edges if target == node), default=0)


def fetch(tiles_hbm, tiles, tile_sem, k):
    cut = pl.ds(k * CUT, CUT)
    return pltpu.make_async_copy(tiles_hbm.at[:, cut], tiles.at[:, cut], tile_sem.at[k])


def half(rows_v, cols_v, count_s, tiles_hbm, tiles, orb, by_block, chosen, tile_sem, copies, slots, placed, flat,
         hx_own, hy_own):
    for copy in copies:
        copy.wait()
    block_id = lax.broadcasted_iota(jnp.int32, (NBP, NT), 0)
    slot_id = lax.broadcasted_iota(jnp.int32, (NBP, NT), 1)
    by_block[...] = jnp.zeros_like(by_block)
    for b in range(NB):
        by_block[:, b, :] = orb[:, b * TILE:(b + 1) * TILE].astype(jnp.float32)
    hot = jnp.where(cols_v[...] == block_id, 1.0, 0.0).astype(jnp.bfloat16)
    for i in range(OL):
        chosen[i] = lax.dot_general(hot, by_block[i].astype(jnp.bfloat16), (((0,), (0,)), ((), ())),
                                    preferred_element_type=jnp.float32)
    for k in range(NT // CUT):
        fetch(tiles_hbm, tiles, tile_sem, k).wait()
        if k + AHEAD < NT // CUT:
            fetch(tiles_hbm, tiles, tile_sem, k + AHEAD).start()
        for t in range(k * CUT, (k + 1) * CUT):
            block = chosen[:, t, :].astype(jnp.bfloat16)
            tile = tiles[:, t].reshape(PD * TILE, TILE)
            got = lax.dot_general(block, tile, (((1,), (1,)), ((), ())), preferred_element_type=jnp.float32)
            for p in range(PD):
                slots[p * OL:(p + 1) * OL, t, :] = got[:, p * TILE:(p + 1) * TILE]
    hot = jnp.where((rows_v[...] == block_id) & (slot_id < count_s[0]), 1.0, 0.0).astype(jnp.bfloat16)
    hot = jnp.concatenate([hot, hot, hot], axis=1)
    for k in range(0, KP, 2):
        parts = []
        for j in (k, k + 1):
            value = slots[j]
            high = value.astype(jnp.bfloat16)
            rest = value - high.astype(jnp.float32)
            middle = rest.astype(jnp.bfloat16)
            low = (rest - middle.astype(jnp.float32)).astype(jnp.bfloat16)
            parts.append(jnp.concatenate([high, middle, low], axis=0))
        sums = jnp.dot(hot, jnp.concatenate(parts, axis=1), preferred_element_type=jnp.float32)
        placed[k] = sums[:, 0:TILE]
        placed[k + 1] = sums[:, TILE:2 * TILE]
    for b in range(NB):
        flat[:, b * TILE:(b + 1) * TILE] = placed[:, b, :]
    for x in range(NX):
        parts = []
        for g in range(NG):
            for o in range(NZ):
                a = o * COLS + x * SEG + START[g]
                parts.append(flat[:, a:a + GROUP[g]])
            if LANES[g] > NZ * GROUP[g]:
                parts.append(jnp.zeros((KP, LANES[g] - NZ * GROUP[g]), jnp.float32))
        hx_own[x] = jnp.concatenate(parts, axis=1).astype(jnp.bfloat16)
    for y in range(NY):
        parts = []
        for c in range(NC):
            for x in range(NX):
                a = ((y * NX + x) * NC + c) * ROWS
                parts.append(flat[:, a:a + ROWS])
            parts.append(jnp.zeros((KP, YH - NX * ROWS), jnp.float32))
        hy_own[y] = jnp.concatenate(parts, axis=1).astype(jnp.bfloat16)


def exchange_kernel(
    rows_hbm, cols_hbm, count_hbm, tiles_hbm, orb_hbm, out_ref,
    rows_v, cols_v, count_s, tiles, orb, by_block, chosen, slots, placed, flat, hx_ref, hy_ref,
    hx, hy, own, sib_out, sib_in, tree_out, tree_in, final_out, final_in,
    local_sem, tile_sem, x_send, x_recv, y_send, y_recv, ring_send, ring_recv, row_send, row_recv,
    sib_send, sib_recv, tree_send, tree_recv, fin_send, fin_recv,
):
    aux = lax.axis_index("aux")
    z = lax.axis_index("occ")
    c = lax.rem(aux, NC)
    x = lax.rem(aux // NC, NX)
    y = aux // (NC * NX)
    sign = 1 - 2 * c

    def at(y_, x_, c_, z_):
        return ((y_ * NX + x_) * NC + c_, z_)

    def xp(d):
        return lax.rem(x + d + NX, NX)

    def yp(d):
        return lax.rem(y + d + NY, NY)

    def zp(d):
        return lax.rem(z + sign * d + NZ, NZ)

    small = [
        pltpu.make_async_copy(rows_hbm, rows_v, local_sem.at[0]),
        pltpu.make_async_copy(cols_hbm, cols_v, local_sem.at[1]),
        pltpu.make_async_copy(count_hbm, count_s, local_sem.at[2]),
        pltpu.make_async_copy(orb_hbm, orb, local_sem.at[3]),
    ]
    for copy in small:
        copy.start()
    for k in range(AHEAD):
        fetch(tiles_hbm, tiles, tile_sem, k).start()
    partners = [at(y, xp(d), c, z) for d in range(1, NX)]
    partners += [at(yp(d), x, c, z) for d in range(1, NY)]
    partners += [at(y, x, c, zp(d)) for d in (1, 2, -1, -2)]
    partners += [at(y, x, 1 - c, z)]
    barrier = pltpu.get_barrier_semaphore()
    for partner in partners:
        pl.semaphore_signal(barrier, inc=1, device_id=partner, device_id_type=MESH)
    half(rows_v, cols_v, count_s, tiles_hbm, tiles, orb, by_block, chosen, tile_sem, small, slots, placed, flat, hx_ref, hy_ref)
    pl.semaphore_wait(barrier, len(partners))

    started = []

    def send(src, dst, s_sem, r_sem, device):
        copy = pltpu.make_async_remote_copy(
            src_ref=src, dst_ref=dst, send_sem=s_sem, recv_sem=r_sem, device_id=device, device_id_type=MESH)
        copy.start()
        started.append(copy)
        return copy

    def arrive(copies):
        for copy in copies:
            copy.wait_recv()

    def hand_out(part, lanes):
        return [send(hx_ref.at[xp(d), :, lanes], hx.at[y, x, :, lanes], x_send.at[part, d - 1], x_recv.at[part, d - 1],
                     at(y, xp(d), c, z)) for d in (1, 3, 2)]

    to_x = [hand_out(0, pl.ds(0, LANES[0])), hand_out(1, pl.ds(LANES[0], XW - LANES[0]))]
    order = (1, 7, 2, 6, 3, 5, 4)
    to_y = {d: send(hy_ref.at[yp(d)], hy.at[y, x], y_send.at[d - 1], y_recv.at[d - 1], at(yp(d), x, c, z))
            for d in order}
    hx[y, x] = hx_ref[x]
    hy[y, x] = hy_ref[y]

    right, left = at(y, xp(1), c, z), at(y, xp(-1), c, z)
    row0, row1 = {}, {}

    def spread(d):
        piece_ref = hy.at[yp(-d), x]
        row0[d] = (send(piece_ref, piece_ref, row_send.at[0, d], row_recv.at[0, d], right),
                   send(piece_ref, piece_ref, row_send.at[1, d], row_recv.at[1, d], left))

    def pass_on(d):
        arrive(row0[d])
        way = d % 2
        piece_ref = hy.at[yp(-d), xp(1 if way else -1)]
        row1[d] = send(piece_ref, piece_ref, row_send.at[2, d], row_recv.at[2, d], left if way else right)

    spread(0)

    rings = {}

    def ring(g, stage):
        lanes = pl.ds(BASE[g], LANES[g])
        count = sum(len(s) for s in GATHER[g][:stage])
        copies = []
        for n, (behind, hops, halved) in enumerate(GATHER[g][stage]):
            for way, turn in ((0, 1), (1, -1)):
                chunk = yp(-turn * behind)
                if halved:
                    ref = hx.at[chunk, 2 * way:2 * way + 2, :, lanes]
                else:
                    ref = hx.at[chunk, :, :, lanes]
                copies.append(send(ref, ref, ring_send.at[way, g, count + n], ring_recv.at[way, g, count + n],
                                   at(yp(turn * hops), x, c, z)))
        rings[g, stage] = copies

    arrive(to_x[0])
    ring(0, 0)
    arrive(to_x[1])
    for g in range(1, NG):
        ring(g, 0)
    for d in order:
        arrive([to_y[d]])
        spread(d)
    arrive(rings[0, 0])
    ring(0, 1)
    for d in (0,) + order[:3]:
        pass_on(d)
    for g in range(1, NG):
        arrive(rings[g, 0])
        ring(g, 1)
    for d in order[3:]:
        pass_on(d)
    for g in range(NG):
        if len(GATHER[g]) > 2:
            arrive(rings[g, 1])
            ring(g, 2)
    arrive(row1.values())

    sibling = at(y, x, 1 - c, z)
    sib = {}

    def product(g, core, j):
        hx_all = hx[:, :, :, BASE[g] + j:BASE[g] + j + TILE].reshape(NY * NX * KP, TILE)
        hy_all = hy[:, :, :, pl.ds(pl.multiple_of(core * YH, TILE), YH)].reshape(NY * NX * KP, YH)
        return lax.dot_general(hx_all, hy_all, (((0,), (0,)), ((), ())), preferred_element_type=jnp.float32)

    def multiply(g):
        used = NZ * GROUP[g]
        for j in range(0, LANES[g], TILE):
            sib_out[g, j:j + TILE, :] = product(g, 1 - c, j).astype(jnp.bfloat16)
        sib[g] = send(sib_out.at[g, 0:used], sib_in.at[g, 0:used], sib_send.at[g], sib_recv.at[g], sibling)
        for j in range(0, LANES[g], TILE):
            own[g, j:j + TILE, :] = product(g, c, j)

    def add_sibling(g):
        used = NZ * GROUP[g]
        sib[g].wait_recv()
        own[g, 0:used, :] += sib_in[g, 0:used, :].astype(jnp.float32)

    trees = {}

    def piece(g, o):
        return own[g, pl.ds(pl.multiple_of(o * GROUP[g], 16), GROUP[g]), :]

    def gathered(g, way, node, value):
        for n, (source, target) in enumerate(EDGES[g][way]):
            if target == node:
                trees[g, way, n].wait_recv()
                value = value + tree_in[g, way, n, 0:GROUP[g], :].astype(jnp.float32)
        return value

    def tree(g, depth):
        for n in range(6):
            for way, turn in ((0, 1), (1, -1)):
                edges = EDGES[g][way]
                if n < len(edges) and level(edges, edges[n][0]) == depth:
                    source, target = edges[n]
                    value = gathered(g, way, source, piece(g, zp(-turn * source)))
                    tree_out[g, way, n, 0:GROUP[g], :] = value.astype(jnp.bfloat16)
                    trees[g, way, n] = send(
                        tree_out.at[g, way, n, 0:GROUP[g]], tree_in.at[g, way, n, 0:GROUP[g]],
                        tree_send.at[g, way, n], tree_recv.at[g, way, n], at(y, x, c, zp(-turn * (source - target))))

    for g in range(NG):
        arrive(rings[g, len(GATHER[g]) - 1])
        multiply(g)
        if g == NG - 2:
            continue
        if g == NG - 1:
            add_sibling(g - 1)
            tree(g - 1, 0)
        add_sibling(g)
        tree(g, 0)
    for depth in (1, 2):
        for g in range(NG):
            tree(g, depth)
    last = []
    for g in range(NG):
        value = piece(g, z)
        for way in range(2):
            value = gathered(g, way, 0, value)
        rows = pl.ds(START[g], GROUP[g])
        for q in range(NX):
            final_out[q, rows, 0:ROWS] = value[:, q * ROWS:(q + 1) * ROWS]
            final_out[q, rows, ROWS:TILE] = jnp.zeros((GROUP[g], TILE - ROWS), jnp.float32)
        last += [send(final_out.at[xp(d), rows], final_in.at[x, rows], fin_send.at[g, d - 1], fin_recv.at[g, d - 1],
                      at(y, xp(d), c, z)) for d in range(1, NX)]
        final_in[x, rows] = final_out[x, rows]
    arrive(last)
    out_ref[...] = final_in[...].reshape(COLS, TILE).T[0:ROWS]
    for copy in started:
        copy.wait_send()


def per_device(aux_tiles, orbitals, tile_rows, tile_cols, tile_count):
    anywhere = pl.BlockSpec(memory_space=pl.ANY)
    dma = pltpu.SemaphoreType.DMA
    f32, bf16 = jnp.float32, jnp.bfloat16
    most = max(LANES)
    return pl.pallas_call(
        exchange_kernel,
        out_shape=jax.ShapeDtypeStruct((ROWS, COLS), f32),
        in_specs=[anywhere] * 5,
        out_specs=pl.BlockSpec(memory_space=pltpu.VMEM),
        scratch_shapes=[
            pltpu.VMEM((1, NT), jnp.int32),
            pltpu.VMEM((1, NT), jnp.int32),
            pltpu.SMEM((1,), jnp.int32),
            pltpu.VMEM((PD, NT, TILE, TILE), bf16),
            pltpu.VMEM((OL, BASIS), bf16),
            pltpu.VMEM((OL, NBP, TILE), f32),
            pltpu.VMEM((OL, NT, TILE), f32),
            pltpu.VMEM((KP, NT, TILE), f32),
            pltpu.VMEM((KP, NBP, TILE), f32),
            pltpu.VMEM((KP, BASIS), f32),
            pltpu.VMEM((NX, KP, XW), bf16),
            pltpu.VMEM((NY, KP, YW), bf16),
            pltpu.VMEM((NY, NX, KP, XW), bf16),
            pltpu.VMEM((NY, NX, KP, YW), bf16),
            pltpu.VMEM((NG, most, YH), f32),
            pltpu.VMEM((NG, most, YH), bf16),
            pltpu.VMEM((NG, most, YH), bf16),
            pltpu.VMEM((NG, 2, 6, max(GROUP), YH), bf16),
            pltpu.VMEM((NG, 2, 6, max(GROUP), YH), bf16),
            pltpu.VMEM((NX, SEG, TILE), f32),
            pltpu.VMEM((NX, SEG, TILE), f32),
            dma((4,)), dma((NT // CUT,)), dma((2, 3)), dma((2, 3)), dma((7,)), dma((7,)),
            dma((2, NG, 4)), dma((2, NG, 4)), dma((3, NY)), dma((3, NY)),
            dma((NG,)), dma((NG,)), dma((NG, 2, 6)), dma((NG, 2, 6)),
            dma((NG, 3)), dma((NG, 3)),
        ],
        compiler_params=pltpu.CompilerParams(
            collective_id=0, has_side_effects=True, vmem_limit_bytes=56 * 2**20),
    )(tile_rows, tile_cols, tile_count, aux_tiles, orbitals)


def solution(mesh):
    return jax.shard_map(
        per_device,
        mesh=mesh,
        in_specs=(
            P("aux", None, None, None),
            P("occ", None),
            P("aux", None),
            P("aux", None),
            P("aux"),
        ),
        out_specs=P("aux", "occ"),
        check_vma=False,
    )
```
